32 devices in a mesh: inl: 8 (over z, y), off: 4 (over x, core).
Axes of the slice: x: 2, y: 2, z: 4, core: 2. Of those that a mesh axis runs over, the one named last changes fastest.
Arguments:
- traces: bfloat16 [4, 4096, 4096], P('off', 'inl'), may hold values from -24 to 24, as said below
- owner: int32 [4, 4096, 1], P('off', 'inl'), may hold values from 0 to 7; in each aligned block of 512 rows (0 to 511, 512 to 1023, ..., all dimensions but the last counted through in order) at most 192 rows name the same one
- local_bin: int32 [4, 4096], P('off', 'inl'), may hold values from 0 to 63
- live_count: int32 [4, 8], P('off', 'inl'), may hold values from 256 to 512, as said below
- xl_gain: float32 [16], replicated, may hold values from 0.2 to 1
- il_gain: float32 [32], replicated, may hold values from 0.2 to 1
Outputs:
- volume: bfloat16 [4, 16, 32, 4096], P('off', 'inl')
The draws below stay inside these ranges and needn't reach their ends.
Inputs may be any that keep to these rules, and one draw needn't show every extreme that they name: `traces`: every trace amplitude lies in this range. Among the traces of one device no owner is named more than 192 times; some device names one owner exactly 192 times. The first live_count traces of a device are live; some device has all 512 traces live.
All inputs are finite; a program needn't handle non-finite values.
Results may differ from the reference program's by a relative error of at most 0.024.
Values may be sent and summed in bfloat16 or wider, within the bound.
A program may use at most 128 MiB of HBM per device.

```python
import math
import jax
import jax.numpy as jnp
import numpy as np
from jax import lax

NS = 4096
NLAG = 80
TR_DEV = 512
IL_DEV = 4
NIL = 32
NXL = 16
BIN_DEV = 64
CAP = 192
TRACES = 4096
N_INL = 8
N_OFF = 4


def draw_traces(key, part):
    keys = jax.random.split(key, 6)
    rows = N_INL * TR_DEV
    shape = (N_OFF, rows, NS)
    noise = jax.random.normal(keys[1], shape, jnp.float32)
    noise = jnp.clip(noise, -6.0, 6.0)
    first = jax.random.uniform(keys[2], (N_OFF, rows, 1), jnp.float32, 0.3, 0.9)
    second = jax.random.uniform(keys[3], (N_OFF, rows, 1), jnp.float32, -0.6, -0.1)
    shifted_one = jnp.pad(noise, ((0, 0), (0, 0), (1, 0)))[:, :, :NS]
    shifted_two = jnp.pad(noise, ((0, 0), (0, 0), (2, 0)))[:, :, :NS]
    colored = noise + first * shifted_one + second * shifted_two
    period = jax.random.randint(keys[4], (N_OFF, rows, 1), NLAG // 2, NLAG)
    moments = jnp.arange(NS, dtype=jnp.int32)[None, None, :] - period
    echo = jnp.where(moments >= 0, jnp.take_along_axis(colored, jnp.maximum(moments, 0), axis=2), 0.0)
    strength = jax.random.uniform(keys[5], (N_OFF, rows, 1), jnp.float32, 0.3, 0.6)
    field = colored - strength * echo
    level = jnp.power(3.0, -jnp.arange(N_OFF, dtype=jnp.float32) / max(N_OFF - 1, 1))
    return (field * level[:, None, None]).astype(jnp.bfloat16)


def draw_live_count(key, part):
    keys = jax.random.split(key, 2)
    shape = (N_OFF, N_INL)
    values = TR_DEV - jax.random.randint(keys[0], shape, 0, TR_DEV // 2 + 1)
    chosen = jax.random.randint(keys[1], (), 0, N_OFF * N_INL)
    places = jnp.arange(N_OFF * N_INL, dtype=jnp.int32).reshape(shape)
    return jnp.where(places == chosen, TR_DEV, values).astype(jnp.int32)


def plant(values, key, smallest, high):
    longest = values.shape.index(max(values.shape))
    spots = []
    for shift in (0, 1):
        where = [jax.random.randint(jax.random.fold_in(key, axis), (), 0, length) for axis, length in enumerate(values.shape)]
        where[longest] = (where[longest] + shift) % values.shape[longest]
        spots.append(tuple(where))
    return values.at[spots[0]].set(smallest).at[spots[1]].set(high)


def deal_out(stream_key, own, number, rows, count, top, most, slope):
    ranking = jax.random.permutation(stream_key, count)
    heavy_load, ordinary = portions_of(count, rows * top, most, slope, True), portions_of(count, rows * top, most, slope, False)
    places = jnp.arange(count)

    def named(sizes, offset_by):
        used = int((sizes > 0).sum())
        fixed = max(1, used // 4)
        passed = fixed + (places - fixed + offset_by * (used - fixed)) % max(1, count - fixed)
        return jnp.zeros((count,), jnp.int32).at[ranking[jnp.where(places < fixed, places, passed)]].set(jnp.asarray(sizes, jnp.int32))

    sizes = jnp.where(number % 4 == 0, named(heavy_load, number // 4), named(ordinary, number - number // 4 - 1))
    mixed = jax.random.permutation(jax.random.fold_in(own, 3), count)
    giver, sink = mixed[0:count // 2 * 2:2], mixed[1:count // 2 * 2:2]
    margin = jnp.minimum(sizes[giver] - 1, most - sizes[sink]) // 2
    margin = jnp.where((giver == ranking[0]) | (sink == ranking[0]) | (sizes[sink] == 0), 0, jnp.maximum(margin, 0))
    passed = jax.random.randint(jax.random.fold_in(own, 4), (count // 2,), 0, 1 << 20) % (margin + 1)
    sizes = sizes.at[giver].add(-passed).at[sink].add(passed)
    items = jnp.searchsorted(jnp.cumsum(sizes), jnp.arange(rows * top), side="right").astype(jnp.int32)
    listing = items.reshape(top, rows).T
    listing = listing[jax.random.permutation(jax.random.fold_in(own, 1), rows)]
    offset_by = jax.random.randint(jax.random.fold_in(own, 2), (rows, 1), 0, top)
    return jnp.take_along_axis(listing, (jnp.arange(top)[None, :] + offset_by) % top, axis=1)


def portions_of(count, total, most, slope, full):
    portions = [(1 << 20) // math.isqrt(standing ** slope) + 1 for standing in range(1, count + 1)]
    largest = most if full else min(most, max(-(-total // count), total * portions[0] // sum(portions)))
    least = 1 if total - largest >= count - 1 else 0
    given, rest = [largest] + [least] * (count - 1), total - largest - least * (count - 1)
    while rest > 0:
        movable = [i for i in range(1, count) if given[i] < largest] or [i for i in range(1, count) if given[i] < most]
        pool, remaining = sum([portions[i] for i in movable]), rest
        for i in movable:
            addition = min(most - given[i], max(1, remaining * portions[i] // pool), rest)
            given[i] = given[i] + addition
            rest = rest - addition
    return np.array(given)


def setup_inputs(seed: int = 0) -> dict:
    splits = jax.random.split(jax.random.key(seed), 7)
    traces = draw_traces(jax.random.fold_in(splits[6], 71), 0)
    owner_keys = jax.random.split(jax.random.fold_in(splits[1], 1), N_OFF * TRACES // TR_DEV)
    owner_turns = jax.random.permutation(jax.random.fold_in(splits[1], 3), N_OFF * TRACES // TR_DEV)
    owner = jax.vmap(lambda own, number: deal_out(jax.random.fold_in(splits[1], 2), own, number, TR_DEV, N_INL, 1, CAP, 2))(owner_keys, owner_turns).reshape((N_OFF, TRACES, 1))
    local_bin = plant(jax.random.randint(splits[2], (N_OFF, TRACES), 0, BIN_DEV), jax.random.fold_in(splits[2], 1), 0, BIN_DEV - 1).astype(jnp.int32)
    live_count = draw_live_count(jax.random.fold_in(splits[6], 71), 0)
    xl_gain = jnp.clip(jnp.exp(jax.random.uniform(splits[4], (NXL,), jnp.float32, math.log(0.2), math.log(1.0))), 0.2, 1.0)
    il_gain = jnp.clip(jnp.exp(jax.random.uniform(splits[5], (NIL,), jnp.float32, math.log(0.2), math.log(1.0))), 0.2, 1.0)
    return dict(traces=traces, owner=owner, local_bin=local_bin, live_count=live_count, xl_gain=xl_gain, il_gain=il_gain)


damping = 0.1


def levinson(series):
    order = series.shape[0]
    error = series[0] + damping
    coeffs = jnp.zeros_like(series).at[0].set(1.0)
    for section in range(1, order):
        partial_sum = jnp.sum(coeffs[:section] * series[section:0:-1], axis=0)
        reflection = -partial_sum / error
        update = coeffs[:section + 1] + reflection * coeffs[section::-1]
        coeffs = coeffs.at[:section + 1].set(update)
        error = error * (1.0 - reflection * reflection)
    return coeffs


def smooth_matrix(gain, reach):
    width = gain.shape[0]
    index = jnp.arange(width)
    distance = jnp.abs(index[:, None] - index[None, :])
    weight = jnp.take(gain, distance) * jnp.exp(-distance.astype(gain.dtype) / reach)
    return (weight / jnp.sum(weight, axis=1, keepdims=True)).astype(jnp.bfloat16)


def reference(traces, owner, local_bin, live_count, xl_gain, il_gain):
    rows = N_INL * TR_DEV
    total_bins = NIL * NXL
    position = jnp.arange(rows, dtype=jnp.int32) % TR_DEV
    limit = jnp.repeat(live_count, TR_DEV, axis=1)
    alive = position[None, :] < limit
    segment = jnp.where(alive, owner[:, :, 0] * BIN_DEV + local_bin, total_bins).astype(jnp.int32)

    def gather_group(pair):
        block_rows, labels = pair
        values = block_rows.astype(jnp.float32)
        spectrum = jnp.fft.rfft(values, n=2 * NS, axis=1)
        power = spectrum.real * spectrum.real + spectrum.imag * spectrum.imag
        lags = jnp.fft.irfft(power, n=2 * NS, axis=1)[:, :NLAG].astype(values.dtype)
        stack_sum = jax.ops.segment_sum(values, labels, total_bins + 1)[:total_bins]
        counts = jax.ops.segment_sum(jnp.ones((rows,), values.dtype), labels, total_bins + 1)[:total_bins]
        lag_sum = jax.ops.segment_sum(lags, labels, total_bins + 1)[:total_bins]
        return stack_sum, counts, lag_sum

    stack_sum, counts, lag_sum = lax.map(gather_group, (traces, segment))
    lag_total = jnp.sum(lag_sum, axis=0)
    stacked = (stack_sum / jnp.maximum(counts, 1.0)[..., None]).astype(jnp.bfloat16)
    rho = lag_total / jnp.maximum(lag_total[:, :1], 1.0)
    filters = levinson(rho.T).T.astype(jnp.bfloat16)
    filter_spec = jnp.fft.rfft(filters.astype(jnp.float32), n=2 * NS, axis=1)
    cross_matrix = smooth_matrix(xl_gain, NXL / 16.0).astype(jnp.float32)
    inline_matrix = smooth_matrix(il_gain, 2.0 * IL_DEV).astype(jnp.float32)

    def finish(group):
        spectrum = jnp.fft.rfft(group.astype(jnp.float32), n=2 * NS, axis=1)
        decon = jnp.fft.irfft(spectrum * filter_spec, n=2 * NS, axis=1)[:, :NS].astype(jnp.bfloat16)
        cube = decon.reshape(NIL, NXL, NS).astype(jnp.float32)
        smoothed = jnp.einsum('xy,iyt->ixt', cross_matrix, cube, precision=lax.Precision.HIGHEST).astype(jnp.bfloat16)
        result = jnp.einsum('ij,jxt->xit', inline_matrix, smoothed.astype(jnp.float32), precision=lax.Precision.HIGHEST)
        return result.astype(jnp.bfloat16)

    return lax.map(finish, stacked)
```

```python
import math

import jax
import jax.numpy as jnp
from jax import lax
from jax.experimental import pallas as pl
from jax.experimental.pallas import tpu as pltpu
from jax.sharding import PartitionSpec as P

NLAG = 80


damping = 0.1


def levinson(series):
    order = series.shape[0]
    error = series[0] + damping
    coeffs = jnp.zeros_like(series).at[0].set(1.0)
    for section in range(1, order):
        partial_sum = jnp.sum(coeffs[:section] * series[section:0:-1], axis=0)
        reflection = -partial_sum / error
        update = coeffs[: section + 1] + reflection * coeffs[section::-1]
        coeffs = coeffs.at[: section + 1].set(update)
        error = error * (1.0 - reflection * reflection)
    return coeffs


def smooth_matrix(gain, reach):
    width = gain.shape[0]
    index = jnp.arange(width)
    distance = jnp.abs(index[:, None] - index[None, :])
    weight = jnp.take(gain, distance) * jnp.exp(-distance.astype(gain.dtype) / reach)
    return (weight / jnp.sum(weight, axis=1, keepdims=True)).astype(jnp.bfloat16)


def lag_kernel(flip_ref, lead_ref, follow_ref, out_ref):
    height, groups, width = lead_ref.shape
    rows = height * groups
    lead = lead_ref[...].reshape(rows, width)
    follow = follow_ref[...].reshape(rows, width)
    both = jnp.concatenate([lead, follow], axis=1)
    turned = lax.dot_general(
        flip_ref[...], lead, (((1,), (1,)), ((), ())), preferred_element_type=jnp.float32
    )
    column = lax.broadcasted_iota(jnp.int32, (width, rows), 1) // groups
    for item in range(height):
        mine = jnp.where(column == item, turned, 0.0).astype(jnp.bfloat16)
        gram = jnp.dot(mine, both, preferred_element_type=jnp.float32)
        sheared = pltpu.roll(gram, width + 1, 1, stride=1, stride_axis=0)
        out_ref[item : item + 1, :] = jnp.sum(sheared[:, :width], axis=0, keepdims=True)


def autocorrelate(block_rows):
    number, samples = block_rows.shape
    groups = samples // 128
    height = 8
    lead = block_rows.reshape(number, groups, 128)
    follow = jnp.pad(block_rows[:, 128:], ((0, 0), (0, 128))).reshape(number, groups, 128)
    flip = jnp.flip(jnp.eye(128, dtype=jnp.bfloat16), axis=0)
    spec = pl.BlockSpec((height, groups, 128), lambda i: (i, 0, 0))
    return pl.pallas_call(
        lag_kernel,
        grid=(number // height,),
        in_specs=[pl.BlockSpec((128, 128), lambda i: (0, 0)), spec, spec],
        out_specs=pl.BlockSpec((height, 128), lambda i: (i, 0)),
        out_shape=jax.ShapeDtypeStruct((number, 128), jnp.float32),
        cost_estimate=pl.CostEstimate(
            flops=number * 2 * 128 * 256 * 256,
            bytes_accessed=number * samples * 4,
            transcendentals=0,
        ),
        compiler_params=pltpu.CompilerParams(vmem_limit_bytes=32 * 1024 * 1024),
    )(flip, lead, follow)


def apply_filter(stacked, filters):
    number, samples = stacked.shape
    taps = filters.shape[1]
    groups = samples // 128
    column = jnp.arange(256)[None, :, None]
    output_pos = jnp.arange(128)[None, None, :]
    lag_index = jnp.arange(taps)[:, None, None]
    table = (column == output_pos + 128 - lag_index).astype(jnp.bfloat16)

    def apply_one_block(pair):
        part_rows, part_filters = pair
        height = part_rows.shape[0]
        kernel = jnp.einsum(
            "nj,jcb->ncb", part_filters, table, preferred_element_type=jnp.float32
        ).astype(jnp.bfloat16)
        padded = jnp.pad(part_rows, ((0, 0), (128, 0))).reshape(height, groups + 1, 128)
        windows = jnp.concatenate([padded[:, :-1], padded[:, 1:]], axis=2)
        result = jnp.einsum("nac,ncb->nab", windows, kernel, preferred_element_type=jnp.float32)
        return result.reshape(height, samples).astype(jnp.bfloat16)

    block = math.gcd(number, 64)
    result = lax.map(
        apply_one_block,
        (
            stacked.reshape(number // block, block, samples),
            filters.reshape(number // block, block, taps),
        ),
    )
    return result.reshape(number, samples)


def shards(traces, owner, local_bin, live_count, xl_gain, il_gain):
    devices = lax.axis_size("inl")
    traces_here = traces.shape[1]
    samples = traces.shape[2]
    shot_rows = traces[0]
    crosslines = xl_gain.shape[0]
    inlines = il_gain.shape[0]
    inline_dev = inlines // devices
    bins_here = inline_dev * crosslines
    slots = max(2, 3 * traces_here // devices)
    by_bin = bins_here <= slots
    destination = owner[0, :, 0]
    local = local_bin[0]
    order = jnp.arange(traces_here, dtype=jnp.int32)
    alive = order < live_count[0, 0]
    if by_bin:
        slots = bins_here
        place = local
    else:
        earlier = (
            (destination[:, None] == destination[None, :])
            & alive[None, :]
            & (order[None, :] < order[:, None])
        )
        place = jnp.sum(earlier.astype(jnp.int32), axis=1)
    target = jnp.where(alive, destination * slots + place, -1)
    rows = devices * slots
    pick = jnp.arange(rows, dtype=jnp.int32)[:, None] == target[None, :]
    packed = jnp.dot(
        pick.astype(jnp.bfloat16), shot_rows, preferred_element_type=jnp.float32
    ).astype(jnp.bfloat16)
    lags = autocorrelate(shot_rows)
    column = jnp.arange(128, dtype=jnp.int32)[None, :]
    lags = jnp.where(column == 127, 1.0, lags)
    lags = jnp.where(column == 126, local[:, None].astype(jnp.float32), lags)
    lag_rows = jnp.dot(
        pick.astype(jnp.float32),
        lags,
        precision=lax.Precision.HIGHEST,
        preferred_element_type=jnp.float32,
    )
    if by_bin:
        arrived = lax.all_to_all(
            packed.reshape(devices, slots, samples), "inl", split_axis=0, concat_axis=0, tiled=True
        )
        stack_sum = jnp.sum(arrived.astype(jnp.float32), axis=0)
        lag_sum = jnp.sum(
            lax.all_to_all(
                lag_rows.reshape(devices, slots, 128), "inl", split_axis=0, concat_axis=0, tiled=True
            ),
            axis=0,
        )
        counts = lag_sum[:, 127]
    else:
        arrived = lax.all_to_all(packed, "inl", split_axis=0, concat_axis=0, tiled=True)
        arrived_lags = lax.all_to_all(lag_rows, "inl", split_axis=0, concat_axis=0, tiled=True)
        arrived_bins = jnp.where(arrived_lags[:, 127] > 0.5, arrived_lags[:, 126], -1.0)
        onehot = arrived_bins[:, None] == jnp.arange(bins_here, dtype=jnp.float32)[None, :]
        counts = jnp.sum(onehot.astype(jnp.float32), axis=0)
        contract = (((0,), (0,)), ((), ()))
        stack_sum = lax.dot_general(
            onehot.astype(jnp.bfloat16), arrived, contract, preferred_element_type=jnp.float32
        )
        lag_sum = lax.dot_general(
            onehot.astype(jnp.float32),
            arrived_lags,
            contract,
            precision=lax.Precision.HIGHEST,
            preferred_element_type=jnp.float32,
        )
    lag_total = lax.psum(lag_sum[:, :NLAG], "off")
    stacked = (stack_sum / jnp.maximum(counts, 1.0)[:, None]).astype(jnp.bfloat16)
    rho = lag_total / jnp.maximum(lag_total[:, :1], 1.0)
    filters = levinson(rho.T).T.astype(jnp.bfloat16)
    decon = apply_filter(stacked, filters)
    cross_matrix = smooth_matrix(xl_gain, crosslines / 16.0)
    smoothed = jnp.einsum(
        "xy,iyt->ixt",
        cross_matrix,
        decon.reshape(inline_dev, crosslines, samples),
        preferred_element_type=jnp.float32,
    ).astype(jnp.bfloat16)
    relaid = lax.all_to_all(smoothed, "inl", split_axis=1, concat_axis=0, tiled=True)
    inline_matrix = smooth_matrix(il_gain, 2.0 * inline_dev)
    result = jnp.einsum(
        "ij,jxt->xit", inline_matrix, relaid, preferred_element_type=jnp.float32
    ).astype(jnp.bfloat16)
    return result[None]


def solution(mesh):
    placed = (
        P("off", "inl", None),
        P("off", "inl", None),
        P("off", "inl"),
        P("off", "inl"),
        P(),
        P(),
    )
    return jax.shard_map(
        shards, mesh=mesh, in_specs=placed, out_specs=P("off", "inl", None, None), check_vma=False
    )
```
